256 devices in a mesh: slab: 32 (over x, z_lo, y), head: 8 (over z_hi, core).
Axes of the slice: x: 4, y: 4, z: 8 (z_hi: 4, z_lo: 2; z = z_hi * 2 + z_lo), core: 2. Of those that a mesh axis runs over, the one named last changes fastest.
Arguments:
- queries: float32 [24576, 2048], P(('slab', 'head')), may hold values from -6 to 6
- key_tokens: float32 [24576, 2048], P(('slab', 'head')), may hold values from -6 to 6
- value_tokens: float32 [24576, 2048], P(('slab', 'head')), may hold values from -6 to 6
- window_reach: int32 [16, 3], replicated, may hold values from 0 to 1, as said below
Outputs:
- attended: float32 [24576, 2048], P(('slab', 'head'))
The draws below stay inside these ranges and needn't reach their ends.
Inputs may be any that keep to these rules, and one draw needn't show every extreme that they name: `window_reach`: at least one head has reach 1 in all three dimensions and at least one has reach 0 in all three.
All inputs are finite; a program needn't handle non-finite values.
Results may differ from the reference program's by a relative error of at most 0.0003.
Values sent between devices are 32-bit elements; how exact they have to be, the bound alone decides.
No kernel may reach another device: no remote copies, remote signals or barrier semaphores. Data moves between devices by JAX's collectives and lax.ppermute only.
A program may use at most 128 MiB of HBM per device.

```python
import jax
import jax.numpy as jnp
from jax import lax

HEADS = 16
HD = 128
TILE = 384
HT = 4
WT = 2
TT = 8
TOKENS = 24576
FEAT = 2048
N_SLAB = 32


def draw_queries(key, part):
    own_key = jax.random.fold_in(key, 11)
    return jnp.clip(jax.random.normal(own_key, (TOKENS, FEAT), jnp.float32), -6.0, 6.0)


def draw_key_tokens(key, part):
    own_key = jax.random.fold_in(key, 17)
    return jnp.clip(jax.random.normal(own_key, (TOKENS, FEAT), jnp.float32), -6.0, 6.0)


def draw_window_reach(key, part):
    own_key = jax.random.fold_in(key, 23)
    key_bits, key_full, key_empty = jax.random.split(own_key, 3)
    reaches = jax.random.randint(key_bits, (HEADS, 3), 0, 2)
    full_head = jax.random.randint(key_full, (), 0, HEADS)
    empty_head = (full_head + jax.random.randint(key_empty, (), 1, HEADS)) % HEADS
    head_ids = jnp.arange(HEADS)[:, None]
    reaches = jnp.where(head_ids == full_head, 1, reaches)
    reaches = jnp.where(head_ids == empty_head, 0, reaches)
    return reaches.astype(jnp.int32)


def levels(stream_key, shape, cuts, smallest, top_value):
    gain = 1.0
    for dim, blocks in cuts:
        steps = jax.random.uniform(jax.random.fold_in(jax.random.fold_in(stream_key, 6), dim), (blocks,), jnp.float32, smallest / len(cuts), top_value / len(cuts))
        gain = gain * jnp.repeat(jnp.exp(steps), shape[dim] // blocks).reshape((-1,) + (1,) * (len(shape) - 1 - dim))
    return gain


def normal_values(stream_key, dims, deviation, limit, cuts=(), held_as=jnp.bfloat16):
    drawn = jax.random.normal(stream_key, dims, jnp.float32) * deviation
    if len(cuts) > 0:
        drawn = levels(stream_key, dims, cuts, -0.22, 0.18) * drawn
    return jnp.clip(drawn, min=-limit, max=limit).astype(held_as)


def setup_inputs(seed: int = 0) -> dict:
    arg_keys = jax.random.split(jax.random.key(seed), 5)
    queries = draw_queries(jax.random.fold_in(arg_keys[4], 71), 0)
    key_tokens = draw_key_tokens(jax.random.fold_in(arg_keys[4], 71), 0)
    value_tokens = normal_values(arg_keys[2], (TOKENS, FEAT), 1.0, 6.0, ((0, 256),), jnp.float32)
    window_reach = draw_window_reach(jax.random.fold_in(arg_keys[4], 71), 0)
    return dict(queries=queries, key_tokens=key_tokens, value_tokens=value_tokens, window_reach=window_reach)


masked_score = -1.0e30


def reference(queries, key_tokens, value_tokens, window_reach):
    row_tok = WT * TILE

    def by_rows(tensor):
        return tensor.reshape(N_SLAB, row_tok, HEADS, HD)

    query_rows = by_rows(queries)
    margin = HT + 1
    padding = ((margin, margin), (0, 0), (0, 0), (0, 0))
    key_padded = jnp.pad(by_rows(key_tokens), padding)
    value_padded = jnp.pad(by_rows(value_tokens), padding)
    width_tile = jnp.arange(row_tok, dtype=jnp.int32) // TILE
    width_gap = jnp.abs(width_tile[:, None] - width_tile[None, :])
    width_ok = width_gap[None, :, :] <= window_reach[:, 2][:, None, None]
    softmax_scale = HD ** -0.5

    def one_row(slab_row):
        tile_time = slab_row // HT
        tile_height = slab_row % HT
        key_parts = []
        value_parts = []
        mask_parts = []
        for step_t in (-1, 0, 1):
            for step_h in (-1, 0, 1):
                start = (slab_row + margin + step_t * HT + step_h).astype(jnp.int32)
                key_parts.append(lax.dynamic_slice_in_dim(key_padded, start, 1, 0)[0])
                value_parts.append(lax.dynamic_slice_in_dim(value_padded, start, 1, 0)[0])
                inside = (tile_time + step_t >= 0) & (tile_time + step_t < TT) & (tile_height + step_h >= 0) & (tile_height + step_h < HT)
                head_ok = inside & (abs(step_t) <= window_reach[:, 0]) & (abs(step_h) <= window_reach[:, 1])
                mask_parts.append(head_ok[:, None, None] & width_ok)
        key_all = jnp.concatenate(key_parts, axis=0)
        value_all = jnp.concatenate(value_parts, axis=0)
        allowed = jnp.concatenate(mask_parts, axis=2)
        scores = jnp.einsum("qhd,khd->hqk", query_rows[slab_row], key_all, precision=lax.Precision.HIGHEST) * softmax_scale
        scores = jnp.where(allowed, scores, masked_score)
        weights = jax.nn.softmax(scores, axis=2)
        result = jnp.einsum("hqk,khd->qhd", weights, value_all, precision=lax.Precision.HIGHEST)
        return result.reshape(row_tok, HEADS * HD)

    attended = lax.map(one_row, jnp.arange(N_SLAB, dtype=jnp.int32))
    return attended.reshape(N_SLAB * row_tok, HEADS * HD)
```

```python
import functools

import jax
import jax.numpy as jnp
import numpy as np
from jax import lax
from jax.experimental import pallas as pl
from jax.experimental.pallas import tpu as pltpu
from jax.sharding import Mesh, PartitionSpec as P

HD = 128
HEADS = 16
BLOCK = 96
SEG = 192
ROW = 384
KEYS = 768
Q_SCALE = float(HD**-0.5 * np.log2(np.e))
LOW = -1e30

AXES = ("x", "zl", "yh", "yl", "zh", "core")
SIZES = (4, 2, 2, 2, 4, 2)
GROUP = ("zl", "yl", "zh")

KEY_ROWS = (
    (0, 0), (0, 1), (1, 0), (1, 1),
    (-1, 0), (-1, 1), (2, 0), (2, 1),
    (0, 2), (1, 2),
    (-1, 2), (2, 2),
)
N_ROWS = len(KEY_ROWS)


def split_hi_lo(value):
    hi = value.astype(jnp.bfloat16)
    lo = (value - hi.astype(jnp.float32)).astype(jnp.bfloat16)
    return hi, lo


def dot_nt(a, b):
    return lax.dot_general(a, b, (((1,), (1,)), ((), ())), preferred_element_type=jnp.float32)


def dot_nn(a, b):
    return lax.dot_general(a, b, (((1,), (0,)), ((), ())), preferred_element_type=jnp.float32)


def attention_kernel(flags, q_hbm, *refs):
    k_refs, v_refs = refs[:10], refs[10:20]
    o_hbm = refs[20]
    q_f, stage, q_b, k_b, v_b, peak, total, acc, q_sem, sem, o_sem = refs[21:]

    def sources(group, row):
        t, h = KEY_ROWS[row]
        out = []
        for side in range(2):
            own, xm, xp, y, yc = group[side * 5 : side * 5 + 5]
            if h < 2:
                out.append(own.at[t, h] if t in (0, 1) else (xm.at[h] if t < 0 else xp.at[h]))
            else:
                out.append(y.at[t] if t in (0, 1) else yc.at[0 if t < 0 else 1])
        return out

    q_copy = pltpu.make_async_copy(q_hbm, q_f, q_sem)
    q_copy.start()
    for row in range(N_ROWS):

        @pl.when(flags[row] != 0)
        def _():
            for which, group in enumerate((k_refs, v_refs)):
                for side, src in enumerate(sources(group, row)):
                    pltpu.make_async_copy(
                        src, stage.at[row, which, side], sem.at[row, which, side]
                    ).start()

    q_copy.wait()
    for i in range(4):
        hi, lo = split_hi_lo(q_f[i] * Q_SCALE)
        q_b[i, :, :HD] = hi
        q_b[i, :, HD:] = lo
    peak[...] = jnp.full(peak.shape, LOW, jnp.float32)
    total[...] = jnp.zeros(total.shape, jnp.float32)
    acc[...] = jnp.zeros(acc.shape, jnp.float32)

    def pair(i, q0, q1, k0, k1):
        rows = pl.ds(q0, q1 - q0)
        q = q_b[i, q0:q1, :]
        kh = k_b[k0:k1, :HD]
        kl = k_b[k0:k1, HD:]
        s = dot_nt(q, jnp.concatenate([kh, kh], axis=1)) + dot_nt(
            q, jnp.concatenate([kl, kl], axis=1)
        )
        old = peak[i, rows, :]
        new = jnp.maximum(old, jnp.max(s, axis=1, keepdims=True))
        p = jnp.exp2(s - new[:, :1])
        alpha = jnp.exp2(old - new)
        part = p[:, :128]
        for c in range(1, (k1 - k0) // 128):
            part = part + p[:, c * 128 : (c + 1) * 128]
        total[i, rows, :] = total[i, rows, :] * alpha + part
        ph, pw = split_hi_lo(p)
        v = v_b[k0:k1, :]
        pv = dot_nn(ph, v) + dot_nn(pw, v)
        acc[i, rows, :] = acc[i, rows, :] * alpha + (pv[:, :HD] + pv[:, HD:])
        peak[i, rows, :] = new

    def row_step(row, carry):
        @pl.when(flags[row] != 0)
        def _():
            for which in range(2):
                for side in range(2):
                    pltpu.make_async_copy(
                        stage.at[row, which, side], stage.at[row, which, side], sem.at[row, which, side]
                    ).wait()
            for side in range(2):
                for w in range(2):
                    dst = pl.ds(w * 2 * SEG + side * SEG, SEG)
                    src = pl.ds(w * SEG, SEG)
                    hi, lo = split_hi_lo(stage[row, 0, side, src, :])
                    k_b[dst, :HD] = hi
                    k_b[dst, HD:] = lo
                    hi, lo = split_hi_lo(stage[row, 1, side, src, :])
                    v_b[dst, :HD] = hi
                    v_b[dst, HD:] = lo

            def q_step(i, carry):
                wanted = flags[N_ROWS + row * 4 + i]

                @pl.when(wanted == 2)
                def _():
                    pair(i, 0, ROW, 0, KEYS)

                @pl.when(wanted == 1)
                def _():
                    pair(i, 0, SEG, 0, 2 * SEG)
                    pair(i, SEG, ROW, 2 * SEG, KEYS)

                return carry

            lax.fori_loop(0, 4, q_step, 0)

        return carry

    lax.fori_loop(0, N_ROWS, row_step, 0)
    for i in range(4):
        denominator = jnp.sum(total[i], axis=1, keepdims=True)
        q_f[i] = acc[i] / denominator
    o_copy = pltpu.make_async_copy(q_f, o_hbm, o_sem)
    o_copy.start()
    o_copy.wait()


def attention(flags, q, keys, values):
    hbm = pl.BlockSpec(memory_space=pl.ANY)
    return pl.pallas_call(
        attention_kernel,
        out_shape=jax.ShapeDtypeStruct((4, ROW, HD), jnp.float32),
        in_specs=[pl.BlockSpec(memory_space=pltpu.SMEM)] + [hbm] * 21,
        out_specs=hbm,
        scratch_shapes=[
            pltpu.VMEM((4, ROW, HD), jnp.float32),
            pltpu.VMEM((N_ROWS, 2, 2, ROW, HD), jnp.float32),
            pltpu.VMEM((4, ROW, 2 * HD), jnp.bfloat16),
            pltpu.VMEM((KEYS, 2 * HD), jnp.bfloat16),
            pltpu.VMEM((KEYS, 2 * HD), jnp.bfloat16),
            pltpu.VMEM((4, ROW, HD), jnp.float32),
            pltpu.VMEM((4, ROW, HD), jnp.float32),
            pltpu.VMEM((4, ROW, HD), jnp.float32),
            pltpu.SemaphoreType.DMA,
            pltpu.SemaphoreType.DMA((N_ROWS, 2, 2)),
            pltpu.SemaphoreType.DMA,
        ],
        compiler_params=pltpu.CompilerParams(vmem_limit_bytes=40 * 1024 * 1024),
        name="tile_attention",
    )(flags, q, *keys, *values)


def body(queries, key_tokens, value_tokens, window_reach):
    x = lax.axis_index("x")
    yh = lax.axis_index("yh")
    yl = lax.axis_index("yl")
    zl = lax.axis_index("zl")
    zh = lax.axis_index("zh")

    def pieces(tensor):
        cut = tensor.reshape(BLOCK, 2, 2, 4, HD)
        flipped = jnp.where(yh == 1, cut[:, ::-1], cut)
        return flipped.transpose(2, 1, 3, 0, 4).reshape(HEADS, BLOCK, HD)

    def regroup(tensor):
        got = lax.all_to_all(pieces(tensor), GROUP, split_axis=0, concat_axis=0, tiled=True)
        return got.reshape(2, 2, ROW, HD)

    head = (yl ^ yh) * 8 + zl * 4 + zh

    pairs_up = [(i, i + 1) for i in range(3)]
    pairs_down = [(i + 1, i) for i in range(3)]
    pairs_core = [(0, 1), (1, 0)]
    pairs_y = [(i, 3 - i) for i in range(4)]

    def swap(tensor):
        return lax.ppermute(tensor, "core", pairs_core)

    def halo(own):
        xm = lax.ppermute(own[1], "x", pairs_up)
        xp = lax.ppermute(own[0], "x", pairs_down)
        edge = lax.dynamic_index_in_dim(own, 1 - yh, 1, keepdims=False)
        y = lax.ppermute(edge, ("yh", "yl"), pairs_y)
        corner = jnp.stack([
            lax.dynamic_index_in_dim(xm, 1 - yh, 0, keepdims=False),
            lax.dynamic_index_in_dim(xp, 1 - yh, 0, keepdims=False),
        ])
        yc = lax.ppermute(corner, ("yh", "yl"), pairs_y)
        mine = (own, xm, xp, y, yc)
        return mine + tuple(swap(part) for part in mine)

    own_k = regroup(key_tokens)
    keys = halo(own_k)
    own_v = regroup(value_tokens)
    values = halo(own_v)
    own_q = regroup(queries)

    reach = lax.dynamic_index_in_dim(window_reach, head, 0, keepdims=False)
    wanted = []
    for t, h in KEY_ROWS:
        exists = (x > 0) if t < 0 else (x < 3) if t > 1 else True
        for qt in range(2):
            for qh in range(2):
                near_t = True if t == qt else (reach[0] > 0 if abs(t - qt) == 1 else False)
                if h == 2:
                    near_h = (reach[1] > 0) & (yh == 1 - qh)
                else:
                    near_h = True if h == qh else reach[1] > 0
                wanted.append(jnp.asarray(exists & near_t & near_h))
    wanted = jnp.stack(wanted).astype(jnp.int32)
    any_row = jnp.max(wanted.reshape(N_ROWS, 4), axis=1)
    flags = jnp.concatenate([any_row, wanted * (1 + reach[2])]).astype(jnp.int32)

    out = attention(flags, own_q.reshape(4, ROW, HD), keys, values)
    back = lax.all_to_all(out.reshape(HEADS, BLOCK, HD), GROUP, split_axis=0, concat_axis=0, tiled=True)
    back = back.reshape(2, 2, 4, BLOCK, HD)
    back = jnp.where(yh == 1, back[:, ::-1], back)
    return back.transpose(3, 1, 0, 2, 4).reshape(BLOCK, HEADS * HD)


def solution(mesh):
    fine = Mesh(mesh.devices.reshape(SIZES), AXES)
    spec = P(AXES, None)
    return jax.shard_map(
        body,
        mesh=fine,
        in_specs=(spec, spec, spec, P()),
        out_specs=spec,
        check_vma=False,
    )
```

```python
import functools

import jax
import jax.numpy as jnp
import numpy as np
from jax import lax
from jax.experimental import pallas as pl
from jax.experimental.pallas import tpu as pltpu
from jax.sharding import Mesh, PartitionSpec as P

HD = 128
HEADS = 16
BLOCK = 96
TILE_SEG = 192
ROW = 384
KEYS = 768
Q_SCALE = float(HD**-0.5 * np.log2(np.e))
LOW = -1e30
COST = 16 * 10**9

AXES = ("x", "zl", "yh", "yl", "zh", "core")
SIZES = (4, 2, 2, 2, 4, 2)
GROUP = ("zl", "yl", "zh")

OWN_ROWS = ((0, 0), (0, 1), (1, 0), (1, 1))
HALO_ROWS = ((-1, 0), (-1, 1), (2, 0), (2, 1), (0, 2), (1, 2), (-1, 2), (2, 2))


def split_hi_lo(value):
    hi = value.astype(jnp.bfloat16)
    lo = (value - hi.astype(jnp.float32)).astype(jnp.bfloat16)
    return hi, lo


def dot_nt(a, b):
    return lax.dot_general(a, b, (((1,), (1,)), ((), ())), preferred_element_type=jnp.float32)


def dot_nn(a, b):
    return lax.dot_general(a, b, (((1,), (0,)), ((), ())), preferred_element_type=jnp.float32)


def row_flags(rows, info):
    in_time, in_height, in_width, x, yh = (info[i] for i in range(5))
    one = jnp.int32(1)
    flags = []
    for t, h in rows:
        exists = (x > 0).astype(jnp.int32) if t < 0 else (x < 3).astype(jnp.int32) if t > 1 else one
        of_row = []
        for qt in range(2):
            for qh in range(2):
                near_t = one if t == qt else (in_time if abs(t - qt) == 1 else jnp.int32(0))
                if h == 2:
                    near_h = in_height * (yh == 1 - qh).astype(jnp.int32)
                else:
                    near_h = one if h == qh else in_height
                of_row.append(exists * near_t * near_h)
        flags.append(of_row)
    return flags, in_width


def attention_kernel(rows, sources, first, n_in, info, *refs):
    n_rows = len(rows)
    n_out = 2 if first else 1
    ins, outs, scratch = refs[:n_in], refs[n_in : n_in + n_out], refs[n_in + n_out :]
    (q_f, stage, q_b, k_b, v_b, peak, total, acc, acc_0, stat_0, s_0, s_1, m_0, m_1, a_0, a_1, twos, ones,
     q_sem, sem, state_sem, out_sem) = scratch
    flags, in_width = row_flags(rows, info)
    wide = in_width != 0

    def load_row(row):
        @pl.when(functools.reduce(jnp.maximum, flags[row]) != 0)
        def _():
            for side, src in enumerate(sources(ins, row)):
                pltpu.make_async_copy(src, stage.at[row, side], sem.at[row, side]).start()

    q_copy = pltpu.make_async_copy(ins[0], q_f, q_sem)
    q_copy.start()
    for row in range(n_rows):
        load_row(row)
    if not first:
        loads = [
            pltpu.make_async_copy(ins[1], acc_0, state_sem.at[0]),
            pltpu.make_async_copy(ins[2], stat_0, state_sem.at[1]),
        ]
        for load in loads:
            load.start()

    n_twos = jnp.int32(0)
    n_ones = jnp.int32(0)
    for row in range(n_rows):
        held = jnp.int32(-1)
        begun = jnp.int32(0)
        for i in range(4):
            use = flags[row][i]
            pair = use * (held >= 0).astype(jnp.int32)
            twos[n_twos] = row * 32 + jnp.maximum(held, 0) * 8 + i * 2 + (1 - begun)
            n_twos = n_twos + pair
            begun = jnp.maximum(begun, pair)
            held = jnp.where(use == 0, held, jnp.where(pair == 1, -1, i))
        ones[n_ones] = row * 32 + jnp.maximum(held, 0) * 8 + (1 - begun)
        n_ones = n_ones + (held >= 0).astype(jnp.int32)
    last = twos[jnp.maximum(n_twos - 1, 0)] & -2
    twos[n_twos] = last
    twos[n_twos + 1] = last

    peak[...] = jnp.full(peak.shape, LOW, jnp.float32)
    total[...] = jnp.zeros(total.shape, jnp.float32)
    acc[...] = jnp.zeros(acc.shape, jnp.float32)

    q_copy.wait()
    for i in range(4):
        hi, lo = split_hi_lo(q_f[i] * Q_SCALE)
        q_b[i, :, :HD] = hi
        q_b[i, :, HD:] = lo

    def prepare(entry):
        @pl.when((entry & 1) != 0)
        def _():
            row = entry >> 5
            for side in range(2):
                pltpu.make_async_copy(stage.at[row, side], stage.at[row, side], sem.at[row, side]).wait()
            for side in range(2):
                for z in range(4):
                    dst = pl.ds((z // 2) * ROW + side * TILE_SEG + (z % 2) * BLOCK, BLOCK)
                    hi, lo = split_hi_lo(stage[row, side, z, 0])
                    k_b[row, dst, :HD] = hi
                    k_b[row, dst, HD:] = lo
                    hi, lo = split_hi_lo(stage[row, side, z, 1])
                    v_b[row, dst, :HD] = hi
                    v_b[row, dst, HD:] = lo

    def queries_of(entry, double):
        return ((entry >> 3) & 3, (entry >> 1) & 3) if double else ((entry >> 3) & 3,)

    def score(entry, double, tile, s, top, alpha):
        q0, q1, k0, k1 = tile
        size = q1 - q0
        row = entry >> 5
        parts = queries_of(entry, double)
        q = jnp.concatenate([q_b[i, q0:q1, :] for i in parts], axis=0)
        q = jnp.concatenate([q, q], axis=1)
        best = None
        for c in range(k0, k1, 128 * 3):
            kh = k_b[row, c : c + 384, :HD]
            kl = k_b[row, c : c + 384, HD:]
            x = dot_nt(q, jnp.concatenate([kh, kh, kl, kl], axis=1))
            s[: len(parts) * size, c : c + 384] = x
            for j in range(3):
                part = x[:, j * 128 : (j + 1) * 128]
                best = part if best is None else jnp.maximum(best, part)
        best = jnp.max(best, axis=1, keepdims=True)
        for n, i in enumerate(parts):
            own = slice(n * size, (n + 1) * size)
            old = peak[i, q0:q1, :]
            new = jnp.maximum(old, best[own])
            alpha[own, :] = jnp.exp2(old - new)
            top[own, :] = new
            peak[i, q0:q1, :] = new

    def gather(entry, double, tile, s, top, alpha):
        q0, q1, k0, k1 = tile
        size = q1 - q0
        row = entry >> 5
        parts = queries_of(entry, double)
        every = slice(0, len(parts) * size)
        high = top[every, :]
        part = None
        ps = []
        for c in range(k0, k1, 128):
            p = jnp.exp2(s[every, c : c + 128] - high)
            part = p if part is None else part + p
            ps.append(p)
        ph, pw = split_hi_lo(jnp.concatenate(ps, axis=1))
        v = v_b[row, k0:k1, :]
        pv = dot_nn(jnp.concatenate([ph, pw], axis=1), jnp.concatenate([v, v], axis=0))
        pv = pv[:, :HD] + pv[:, HD:]
        for n, i in enumerate(parts):
            own = slice(n * size, (n + 1) * size)
            scale = alpha[own, :]
            total[i, q0:q1, :] = total[i, q0:q1, :] * scale + part[own]
            acc[i, q0:q1, :] = acc[i, q0:q1, :] * scale + pv[own]

    even, odd = (s_0, m_0, a_0), (s_1, m_1, a_1)
    whole = (0, ROW, 0, KEYS)
    halves = [(w * TILE_SEG, (w + 1) * TILE_SEG, w * ROW, (w + 1) * ROW) for w in range(2)]

    @pl.when(wide & (n_twos > 0))
    def _():
        prepare(twos[0])
        score(twos[0], True, whole, *even)

        def step(g, carry):
            n = 2 * g
            here, then, later = twos[n], twos[n + 1], twos[n + 2]
            prepare(then)
            score(then, True, whole, *odd)
            gather(here, True, whole, *even)

            @pl.when(n + 1 < n_twos)
            def _():
                prepare(later)
                score(later, True, whole, *even)
                gather(then, True, whole, *odd)

            return carry

        lax.fori_loop(0, (n_twos + 1) >> 1, step, 0)

    @pl.when(wide)
    def _():
        def step(n, carry):
            here = ones[n]
            prepare(here)
            score(here, False, whole, *even)
            gather(here, False, whole, *even)
            return carry

        lax.fori_loop(0, n_ones, step, 0)

    @pl.when(jnp.logical_not(wide))
    def _():
        for entries, number, double in ((twos, n_twos, True), (ones, n_ones, False)):

            def step(n, carry):
                here = entries[n]
                prepare(here)
                for half, buffers in zip(halves, (even, odd)):
                    score(here, double, half, *buffers)
                for half, buffers in zip(halves, (even, odd)):
                    gather(here, double, half, *buffers)
                return carry

            lax.fori_loop(0, number, step, 0)

    def out_copies(i):
        if first:
            return [
                pltpu.make_async_copy(acc.at[i], outs[0].at[i], out_sem.at[0, i]),
                pltpu.make_async_copy(stat_0.at[i], outs[1].at[i], out_sem.at[1, i]),
            ]
        return [pltpu.make_async_copy(q_f.at[i], outs[0].at[i], out_sem.at[0, i])]

    if not first:
        for load in loads:
            load.wait()
    for i in range(4):
        weight = jnp.sum(total[i], axis=1, keepdims=True)
        if first:
            lane = lax.broadcasted_iota(jnp.int32, (ROW, HD), 1)
            stat_0[i] = jnp.where(lane < HD // 2, peak[i], weight)
        else:
            old = stat_0[i, :, :1]
            here = peak[i, :, :1]
            high = jnp.maximum(old, here)
            scale_0 = jnp.exp2(old - high)
            scale_1 = jnp.exp2(here - high)
            bottom = stat_0[i, :, HD // 2 : HD // 2 + 1] * scale_0 + weight * scale_1
            q_f[i] = (acc_0[i] * scale_0 + acc[i] * scale_1) / bottom
        for copy in out_copies(i):
            copy.start()
    for i in range(4):
        for copy in out_copies(i):
            copy.wait()


def attention(rows, sources, first, info, *arrays):
    n_rows = len(rows)
    hbm = pl.BlockSpec(memory_space=pl.ANY)
    n_out = 2 if first else 1
    state = pltpu.VMEM((4, ROW, HD), jnp.float32)
    column = pltpu.VMEM((2 * ROW, HD), jnp.float32)
    scores = pltpu.VMEM((2 * ROW, KEYS), jnp.float32)
    return pl.pallas_call(
        functools.partial(attention_kernel, rows, sources, first, len(arrays)),
        out_shape=[jax.ShapeDtypeStruct((4, ROW, HD), jnp.float32)] * n_out,
        in_specs=[pl.BlockSpec(memory_space=pltpu.SMEM)] + [hbm] * len(arrays),
        out_specs=[hbm] * n_out,
        scratch_shapes=[
            state,
            pltpu.VMEM((n_rows, 2, 4, 2, BLOCK, HD), jnp.float32),
            pltpu.VMEM((4, ROW, 2 * HD), jnp.bfloat16),
            pltpu.VMEM((n_rows, KEYS, 2 * HD), jnp.bfloat16),
            pltpu.VMEM((n_rows, KEYS, 2 * HD), jnp.bfloat16),
            state,
            state,
            state,
            state,
            state,
            scores,
            scores,
            column,
            column,
            column,
            column,
            pltpu.SMEM((n_rows * 2 + 2,), jnp.int32),
            pltpu.SMEM((n_rows + 1,), jnp.int32),
            pltpu.SemaphoreType.DMA,
            pltpu.SemaphoreType.DMA((n_rows, 2)),
            pltpu.SemaphoreType.DMA((2,)),
            pltpu.SemaphoreType.DMA((2, 4)),
        ],
        compiler_params=pltpu.CompilerParams(vmem_limit_bytes=48 * 1024 * 1024),
        cost_estimate=pl.CostEstimate(flops=COST, bytes_accessed=8 * 2**20, transcendentals=0),
        name="own_rows" if first else "halo_rows",
    )(info, *arrays)


def own_sources(ins, row):
    t, h = OWN_ROWS[row]
    return [ins[1 + side].at[t, h] for side in range(2)]


def halo_sources(ins, row):
    t, h = HALO_ROWS[row]
    out = []
    for side in range(2):
        xm, xp, y, cm, cp = ins[3 + side * 5 : 8 + side * 5]
        if h < 2:
            out.append(xm.at[h] if t < 0 else xp.at[h])
        else:
            out.append(y.at[t] if t in (0, 1) else (cm if t < 0 else cp))
    return out


def body(queries, key_tokens, value_tokens, window_reach):
    yh = lax.axis_index("yh")
    head = (lax.axis_index("yl") ^ yh) * 8 + lax.axis_index("zl") * 4 + lax.axis_index("zh")
    reach = lax.dynamic_slice_in_dim(window_reach, head, 1, 0)[0]
    info = jnp.concatenate([jnp.minimum(reach, 1), jnp.stack([lax.axis_index("x"), yh])])

    def pieces(tensor):
        cut = tensor.reshape(BLOCK, 2, 2, 4, HD)
        flipped = jnp.where(yh == 1, cut[:, ::-1], cut)
        return flipped.transpose(2, 1, 3, 0, 4).reshape(HEADS, BLOCK, HD)

    def exchange(tensor):
        return lax.all_to_all(tensor, GROUP, split_axis=0, concat_axis=0, tiled=True)

    def swap(tensor):
        return lax.ppermute(tensor, "core", [(0, 1), (1, 0)])

    up = [(i, i + 1) for i in range(3)]
    down = [(i + 1, i) for i in range(3)]
    across = [(i, 3 - i) for i in range(4)]

    both = jnp.stack([pieces(key_tokens), pieces(value_tokens)], axis=1)
    own, to_send, info = lax.optimization_barrier((exchange(both), pieces(queries), info))
    own = own.reshape(2, 2, 4, 2, BLOCK, HD)
    own_q = exchange(to_send).reshape(4, ROW, HD)

    xm = lax.ppermute(own[1], "x", up)
    xp = lax.ppermute(own[0], "x", down)
    edge = lax.dynamic_index_in_dim(own, 1 - yh, 1, keepdims=False)
    y = lax.ppermute(edge, ("yh", "yl"), across)
    edge_up = [(i * 4 + j, (i + 1) * 4 + 3 - j) for i in range(3) for j in range(4)]
    edge_down = [((i + 1) * 4 + j, i * 4 + 3 - j) for i in range(3) for j in range(4)]
    cm = lax.ppermute(edge[1], ("x", "yh", "yl"), edge_up)
    cp = lax.ppermute(edge[0], ("x", "yh", "yl"), edge_down)
    halo = (xm, xp, y, cm, cp)
    state = attention(OWN_ROWS, own_sources, True, info, own_q, own, swap(own))
    state, halo = lax.optimization_barrier((state, halo))
    halo = halo + tuple(swap(part) for part in halo)
    (out,) = attention(HALO_ROWS, halo_sources, False, info, own_q, *state, *halo)
    back = exchange(out.reshape(HEADS, BLOCK, HD)).reshape(2, 2, 4, BLOCK, HD)
    back = jnp.where(yh == 1, back[:, ::-1], back)
    return back.transpose(3, 1, 0, 2, 4).reshape(BLOCK, HEADS * HD)


def solution(mesh):
    fine = Mesh(mesh.devices.reshape(SIZES), AXES)
    spec = P(AXES, None)
    return jax.shard_map(
        body,
        mesh=fine,
        in_specs=(spec, spec, spec, P()),
        out_specs=spec,
        check_vma=False,
    )
```

```python
import functools

import jax
import jax.numpy as jnp
import numpy as np
from jax import lax
from jax.experimental import pallas as pl
from jax.experimental.pallas import tpu as pltpu
from jax.sharding import Mesh, PartitionSpec as P

HD = 128
HEADS = 16
BLOCK = 96
TILE_SEG = 192
ROW = 384
KEYS = 768
Q_SCALE = float(HD**-0.5 * np.log2(np.e))
LOW = -1e30
COST = 16 * 10**9

AXES = ("x", "zl", "yh", "yl", "zh", "core")
SIZES = (4, 2, 2, 2, 4, 2)
GROUP = ("zl", "yl", "zh")

OWN_ROWS = ((0, 0), (0, 1), (1, 0), (1, 1))
HALO_ROWS = ((-1, 0), (-1, 1), (2, 0), (2, 1), (0, 2), (1, 2), (-1, 2), (2, 2))


def split_hi_lo(value):
    hi = value.astype(jnp.bfloat16)
    lo = (value - hi.astype(jnp.float32)).astype(jnp.bfloat16)
    return hi, lo


def dot_nt(a, b):
    return lax.dot_general(a, b, (((1,), (1,)), ((), ())), preferred_element_type=jnp.float32)


def dot_nn(a, b):
    return lax.dot_general(a, b, (((1,), (0,)), ((), ())), preferred_element_type=jnp.float32)


def row_flags(rows, info):
    in_time, in_height, in_width, x, yh = (info[i] for i in range(5))
    one = jnp.int32(1)
    flags = []
    for t, h in rows:
        exists = (x > 0).astype(jnp.int32) if t < 0 else (x < 3).astype(jnp.int32) if t > 1 else one
        of_row = []
        for qt in range(2):
            for qh in range(2):
                near_t = one if t == qt else (in_time if abs(t - qt) == 1 else jnp.int32(0))
                if h == 2:
                    near_h = in_height * (yh == 1 - qh).astype(jnp.int32)
                else:
                    near_h = one if h == qh else in_height
                of_row.append(exists * near_t * near_h)
        flags.append(of_row)
    return flags, in_width


def attention_kernel(rows, sources, first, n_in, info, *refs):
    n_rows = len(rows)
    n_out = 2 if first else 1
    ins, outs, scratch = refs[:n_in], refs[n_in : n_in + n_out], refs[n_in + n_out :]
    (q_f, q_b, k_b, v_b, peak, total, acc, acc_0, stat_0, s_0, s_1, m_0, m_1, a_0, a_1, twos, ones,
     q_sem, state_sem, out_sem) = scratch
    flags, in_width = row_flags(rows, info)
    wide = in_width != 0

    q_copy = pltpu.make_async_copy(ins[0], q_f, q_sem)
    q_copy.start()
    if not first:
        loads = [
            pltpu.make_async_copy(ins[1], acc_0, state_sem.at[0]),
            pltpu.make_async_copy(ins[2], stat_0, state_sem.at[1]),
        ]
        for load in loads:
            load.start()

    n_twos = jnp.int32(0)
    n_ones = jnp.int32(0)
    for row in range(n_rows):
        held = jnp.int32(-1)
        begun = jnp.int32(0)
        for i in range(4):
            use = flags[row][i]
            pair = use * (held >= 0).astype(jnp.int32)
            twos[n_twos] = row * 32 + jnp.maximum(held, 0) * 8 + i * 2 + (1 - begun)
            n_twos = n_twos + pair
            begun = jnp.maximum(begun, pair)
            held = jnp.where(use == 0, held, jnp.where(pair == 1, -1, i))
        ones[n_ones] = row * 32 + jnp.maximum(held, 0) * 8 + (1 - begun)
        n_ones = n_ones + (held >= 0).astype(jnp.int32)
    last = twos[jnp.maximum(n_twos - 1, 0)] & -2
    twos[n_twos] = last
    twos[n_twos + 1] = last

    peak[...] = jnp.full(peak.shape, LOW, jnp.float32)
    total[...] = jnp.zeros(total.shape, jnp.float32)
    acc[...] = jnp.zeros(acc.shape, jnp.float32)

    q_copy.wait()
    for i in range(4):
        hi, lo = split_hi_lo(q_f[i] * Q_SCALE)
        q_b[i, :, :HD] = hi
        q_b[i, :, HD:] = lo

    def prepare(entry):
        @pl.when((entry & 1) != 0)
        def _():
            row = entry >> 5
            for r in range(n_rows):

                @pl.when(row == r)
                def _():
                    for side, src in enumerate(sources(ins, r)):
                        for z in range(4):
                            start = (z // 2) * ROW + side * TILE_SEG + (z % 2) * BLOCK
                            hi, lo = split_hi_lo(src[z, 0])
                            k_b[r, start : start + BLOCK, :HD] = hi
                            k_b[r, start : start + BLOCK, HD:] = lo
                            hi, lo = split_hi_lo(src[z, 1])
                            v_b[r, start : start + BLOCK, :HD] = hi
                            v_b[r, start : start + BLOCK, HD:] = lo

    def queries_of(entry, double):
        return ((entry >> 3) & 3, (entry >> 1) & 3) if double else ((entry >> 3) & 3,)

    def score(entry, double, tile, s, top, alpha):
        q0, q1, k0, k1 = tile
        size = q1 - q0
        row = entry >> 5
        parts = queries_of(entry, double)
        q = jnp.concatenate([q_b[i, q0:q1, :] for i in parts], axis=0)
        q = jnp.concatenate([q, q], axis=1)
        best = None
        for c in range(k0, k1, 128 * 3):
            kh = k_b[row, c : c + 384, :HD]
            kl = k_b[row, c : c + 384, HD:]
            x = dot_nt(q, jnp.concatenate([kh, kh, kl, kl], axis=1))
            s[: len(parts) * size, c : c + 384] = x
            for j in range(3):
                part = x[:, j * 128 : (j + 1) * 128]
                best = part if best is None else jnp.maximum(best, part)
        best = jnp.max(best, axis=1, keepdims=True)
        for n, i in enumerate(parts):
            own = slice(n * size, (n + 1) * size)
            old = peak[i, q0:q1, :]
            new = jnp.maximum(old, best[own])
            alpha[own, :] = jnp.exp2(old - new)
            top[own, :] = new
            peak[i, q0:q1, :] = new

    def gather(entry, double, tile, s, top, alpha):
        q0, q1, k0, k1 = tile
        size = q1 - q0
        row = entry >> 5
        parts = queries_of(entry, double)
        every = slice(0, len(parts) * size)
        high = top[every, :]
        part = None
        ps = []
        for c in range(k0, k1, 128):
            p = jnp.exp2(s[every, c : c + 128] - high)
            part = p if part is None else part + p
            ps.append(p)
        ph, pw = split_hi_lo(jnp.concatenate(ps, axis=1))
        v = v_b[row, k0:k1, :]
        pv = dot_nn(jnp.concatenate([ph, pw], axis=1), jnp.concatenate([v, v], axis=0))
        pv = pv[:, :HD] + pv[:, HD:]
        for n, i in enumerate(parts):
            own = slice(n * size, (n + 1) * size)
            scale = alpha[own, :]
            total[i, q0:q1, :] = total[i, q0:q1, :] * scale + part[own]
            acc[i, q0:q1, :] = acc[i, q0:q1, :] * scale + pv[own]

    even, odd = (s_0, m_0, a_0), (s_1, m_1, a_1)
    whole = (0, ROW, 0, KEYS)
    halves = [(w * TILE_SEG, (w + 1) * TILE_SEG, w * ROW, (w + 1) * ROW) for w in range(2)]

    @pl.when(wide & (n_twos > 0))
    def _():
        prepare(twos[0])
        score(twos[0], True, whole, *even)

        def step(g, carry):
            n = 2 * g
            here, then, later = twos[n], twos[n + 1], twos[n + 2]
            prepare(then)
            score(then, True, whole, *odd)
            gather(here, True, whole, *even)

            @pl.when(n + 1 < n_twos)
            def _():
                prepare(later)
                score(later, True, whole, *even)
                gather(then, True, whole, *odd)

            return carry

        lax.fori_loop(0, (n_twos + 1) >> 1, step, 0)

    @pl.when(wide)
    def _():
        def step(n, carry):
            here = ones[n]
            prepare(here)
            score(here, False, whole, *even)
            gather(here, False, whole, *even)
            return carry

        lax.fori_loop(0, n_ones, step, 0)

    @pl.when(jnp.logical_not(wide))
    def _():
        for entries, number, double in ((twos, n_twos, True), (ones, n_ones, False)):

            def step(n, carry):
                here = entries[n]
                prepare(here)
                for half, buffers in zip(halves, (even, odd)):
                    score(here, double, half, *buffers)
                for half, buffers in zip(halves, (even, odd)):
                    gather(here, double, half, *buffers)
                return carry

            lax.fori_loop(0, number, step, 0)

    def out_copies(i):
        if first:
            return [
                pltpu.make_async_copy(acc.at[i], outs[0].at[i], out_sem.at[0, i]),
                pltpu.make_async_copy(stat_0.at[i], outs[1].at[i], out_sem.at[1, i]),
            ]
        return [pltpu.make_async_copy(q_f.at[i], outs[0].at[i], out_sem.at[0, i])]

    if not first:
        for load in loads:
            load.wait()
    for i in range(4):
        weight = jnp.sum(total[i], axis=1, keepdims=True)
        if first:
            lane = lax.broadcasted_iota(jnp.int32, (ROW, HD), 1)
            stat_0[i] = jnp.where(lane < HD // 2, peak[i], weight)
        else:
            old = stat_0[i, :, :1]
            here = peak[i, :, :1]
            high = jnp.maximum(old, here)
            scale_0 = jnp.exp2(old - high)
            scale_1 = jnp.exp2(here - high)
            bottom = stat_0[i, :, HD // 2 : HD // 2 + 1] * scale_0 + weight * scale_1
            q_f[i] = (acc_0[i] * scale_0 + acc[i] * scale_1) / bottom
        for copy in out_copies(i):
            copy.start()
    for i in range(4):
        for copy in out_copies(i):
            copy.wait()


def attention(rows, sources, first, info, *arrays):
    n_rows = len(rows)
    hbm = pl.BlockSpec(memory_space=pl.ANY)
    n_out = 2 if first else 1
    state = pltpu.VMEM((4, ROW, HD), jnp.float32)
    column = pltpu.VMEM((2 * ROW, HD), jnp.float32)
    scores = pltpu.VMEM((2 * ROW, KEYS), jnp.float32)
    return pl.pallas_call(
        functools.partial(attention_kernel, rows, sources, first, len(arrays)),
        out_shape=[jax.ShapeDtypeStruct((4, ROW, HD), jnp.float32)] * n_out,
        in_specs=[pl.BlockSpec(memory_space=pltpu.SMEM)]
        + [hbm] * (1 if first else 3)
        + [pl.BlockSpec(memory_space=pltpu.VMEM)] * (len(arrays) - (1 if first else 3)),
        out_specs=[hbm] * n_out,
        scratch_shapes=[
            state,
            pltpu.VMEM((4, ROW, 2 * HD), jnp.bfloat16),
            pltpu.VMEM((n_rows, KEYS, 2 * HD), jnp.bfloat16),
            pltpu.VMEM((n_rows, KEYS, 2 * HD), jnp.bfloat16),
            state,
            state,
            state,
            state,
            state,
            scores,
            scores,
            column,
            column,
            column,
            column,
            pltpu.SMEM((n_rows * 2 + 2,), jnp.int32),
            pltpu.SMEM((n_rows + 1,), jnp.int32),
            pltpu.SemaphoreType.DMA,
            pltpu.SemaphoreType.DMA((2,)),
            pltpu.SemaphoreType.DMA((2, 4)),
        ],
        compiler_params=pltpu.CompilerParams(vmem_limit_bytes=(24 if first else 28) * 1024 * 1024),
        cost_estimate=pl.CostEstimate(flops=COST, bytes_accessed=8 * 2**20, transcendentals=0),
        name="own_rows" if first else "halo_rows",
    )(info, *arrays[: 1 if first else 3], *[pltpu.with_memory_space_constraint(x, pltpu.VMEM) for x in arrays[1 if first else 3 :]])


def own_sources(ins, row):
    t, h = OWN_ROWS[row]
    return [ins[1 + side].at[t, h] for side in range(2)]


def halo_sources(ins, row):
    t, h = HALO_ROWS[row]
    out = []
    for side in range(2):
        xm, xp, y, cm, cp = ins[3 + side * 5 : 8 + side * 5]
        if h < 2:
            out.append(xm.at[h] if t < 0 else xp.at[h])
        else:
            out.append(y.at[t] if t in (0, 1) else (cm if t < 0 else cp))
    return out


def body(queries, key_tokens, value_tokens, window_reach):
    yh = lax.axis_index("yh")
    head = (lax.axis_index("yl") ^ yh) * 8 + lax.axis_index("zl") * 4 + lax.axis_index("zh")
    reach = lax.dynamic_slice_in_dim(window_reach, head, 1, 0)[0]
    info = jnp.concatenate([jnp.minimum(reach, 1), jnp.stack([lax.axis_index("x"), yh])])

    def pieces(tensor):
        cut = tensor.reshape(BLOCK, 2, 2, 4, HD)
        flipped = jnp.where(yh == 1, cut[:, ::-1], cut)
        return flipped.transpose(2, 1, 3, 0, 4).reshape(HEADS, BLOCK, HD)

    def exchange(tensor):
        return lax.all_to_all(tensor, GROUP, split_axis=0, concat_axis=0, tiled=True)

    def swap(tensor):
        return lax.ppermute(tensor, "core", [(0, 1), (1, 0)])

    up = [(i, i + 1) for i in range(3)]
    down = [(i + 1, i) for i in range(3)]
    across = [(i, 3 - i) for i in range(4)]

    both = jnp.stack([pieces(key_tokens), pieces(value_tokens)], axis=1)
    own, to_send, info = lax.optimization_barrier((exchange(both), pieces(queries), info))
    own = own.reshape(2, 2, 4, 2, BLOCK, HD)
    own_q = exchange(to_send).reshape(4, ROW, HD)

    xm = lax.ppermute(own[1], "x", up)
    xp = lax.ppermute(own[0], "x", down)
    edge = lax.dynamic_index_in_dim(own, 1 - yh, 1, keepdims=False)
    y = lax.ppermute(edge, ("yh", "yl"), across)
    edge_up = [(i * 4 + j, (i + 1) * 4 + 3 - j) for i in range(3) for j in range(4)]
    edge_down = [((i + 1) * 4 + j, i * 4 + 3 - j) for i in range(3) for j in range(4)]
    cm = lax.ppermute(edge[1], ("x", "yh", "yl"), edge_up)
    cp = lax.ppermute(edge[0], ("x", "yh", "yl"), edge_down)
    halo = (xm, xp, y, cm, cp)
    state = attention(OWN_ROWS, own_sources, True, info, own_q, own, swap(own))
    state, halo = lax.optimization_barrier((state, halo))
    halo = halo + tuple(swap(part) for part in halo)
    (out,) = attention(HALO_ROWS, halo_sources, False, info, own_q, *state, *halo)
    back = exchange(out.reshape(HEADS, BLOCK, HD)).reshape(2, 2, 4, BLOCK, HD)
    back = jnp.where(yh == 1, back[:, ::-1], back)
    return back.transpose(3, 1, 0, 2, 4).reshape(BLOCK, HEADS * HD)


def solution(mesh):
    fine = Mesh(mesh.devices.reshape(SIZES), AXES)
    spec = P(AXES, None)
    return jax.shard_map(
        body,
        mesh=fine,
        in_specs=(spec, spec, spec, P()),
        out_specs=spec,
        check_vma=False,
    )
```

```python
import functools

import jax
import jax.numpy as jnp
import numpy as np
from jax import lax
from jax.experimental import pallas as pl
from jax.experimental.pallas import tpu as pltpu
from jax.sharding import Mesh, PartitionSpec as P

HD = 128
HEADS = 16
BLOCK = 96
TILE_SEG = 192
ROW = 384
KEYS = 768
Q_SCALE = float(HD**-0.5 * np.log2(np.e))
LOW = -1e30
COST = 16 * 10**9

AXES = ("x", "zl", "yh", "yl", "zh", "core")
SIZES = (4, 2, 2, 2, 4, 2)
GROUP = ("yh", "zl", "yl", "zh")
RANKS = [
    [((yh * 2 + zl) * 2 + (yl ^ yh)) * 4 + zh for zl in range(2) for yl in range(2) for zh in range(4)]
    for yh in range(2)
]

OWN_ROWS = ((0, 0), (0, 1), (1, 0), (1, 1))
HALO_ROWS = ((-1, 0), (-1, 1), (2, 0), (2, 1), (0, 2), (1, 2), (-1, 2), (2, 2))


def split_hi_lo(value):
    hi = value.astype(jnp.bfloat16)
    lo = (value - hi.astype(jnp.float32)).astype(jnp.bfloat16)
    return hi, lo


def dot_nt(a, b):
    return lax.dot_general(a, b, (((1,), (1,)), ((), ())), preferred_element_type=jnp.float32)


def dot_nn(a, b):
    return lax.dot_general(a, b, (((1,), (0,)), ((), ())), preferred_element_type=jnp.float32)


def row_flags(rows, info):
    in_time, in_height, in_width, x = (info[i] for i in range(4))
    one = jnp.int32(1)
    flags = []
    for t, h in rows:
        exists = (x > 0).astype(jnp.int32) if t < 0 else (x < 3).astype(jnp.int32) if t > 1 else one
        of_row = []
        for qt in range(2):
            for qh in range(2):
                near_t = one if t == qt else (in_time if abs(t - qt) == 1 else jnp.int32(0))
                if h == 2:
                    near_h = in_height if qh == 1 else jnp.int32(0)
                else:
                    near_h = one if h == qh else in_height
                of_row.append(exists * near_t * near_h)
        flags.append(of_row)
    return flags, in_width


def attention_kernel(rows, sources, first, n_in, info, *refs):
    n_rows = len(rows)
    n_out = 2 if first else 1
    ins, outs, scratch = refs[:n_in], refs[n_in : n_in + n_out], refs[n_in + n_out :]
    (q_f, q_b, k_b, v_b, peak, total, acc, acc_0, stat_0, s_0, s_1, m_0, m_1, a_0, a_1, twos, ones,
     q_sem, state_sem, out_sem) = scratch
    flags, in_width = row_flags(rows, info)
    wide = in_width != 0

    q_copy = pltpu.make_async_copy(ins[0], q_f, q_sem)
    q_copy.start()
    if not first:
        loads = [
            pltpu.make_async_copy(ins[1], acc_0, state_sem.at[0]),
            pltpu.make_async_copy(ins[2], stat_0, state_sem.at[1]),
        ]
        for load in loads:
            load.start()

    n_twos = jnp.int32(0)
    n_ones = jnp.int32(0)
    for row in range(n_rows):
        held = jnp.int32(-1)
        begun = jnp.int32(0)
        for i in range(4):
            use = flags[row][i]
            pair = use * (held >= 0).astype(jnp.int32)
            twos[n_twos] = row * 32 + jnp.maximum(held, 0) * 8 + i * 2 + (1 - begun)
            n_twos = n_twos + pair
            begun = jnp.maximum(begun, pair)
            held = jnp.where(use == 0, held, jnp.where(pair == 1, -1, i))
        ones[n_ones] = row * 32 + jnp.maximum(held, 0) * 8 + (1 - begun)
        n_ones = n_ones + (held >= 0).astype(jnp.int32)
    last = twos[jnp.maximum(n_twos - 1, 0)] & -2
    twos[n_twos] = last
    twos[n_twos + 1] = last

    peak[...] = jnp.full(peak.shape, LOW, jnp.float32)
    total[...] = jnp.zeros(total.shape, jnp.float32)
    acc[...] = jnp.zeros(acc.shape, jnp.float32)

    q_copy.wait()
    for i in range(4):
        hi, lo = split_hi_lo(q_f[i] * Q_SCALE)
        q_b[i, :, :HD] = hi
        q_b[i, :, HD:] = lo

    def prepare(entry):
        @pl.when((entry & 1) != 0)
        def _():
            row = entry >> 5
            for r in range(n_rows):

                @pl.when(row == r)
                def _():
                    for side, src in enumerate(sources(ins, r)):
                        for z in range(4):
                            start = (z // 2) * ROW + side * TILE_SEG + (z % 2) * BLOCK
                            hi, lo = split_hi_lo(src[z, 0])
                            k_b[r, start : start + BLOCK, :HD] = hi
                            k_b[r, start : start + BLOCK, HD:] = lo
                            hi, lo = split_hi_lo(src[z, 1])
                            v_b[r, start : start + BLOCK, :HD] = hi
                            v_b[r, start : start + BLOCK, HD:] = lo

    def queries_of(entry, double):
        return ((entry >> 3) & 3, (entry >> 1) & 3) if double else ((entry >> 3) & 3,)

    def score(entry, double, tile, s, top, alpha):
        q0, q1, k0, k1 = tile
        size = q1 - q0
        row = entry >> 5
        parts = queries_of(entry, double)
        q = jnp.concatenate([q_b[i, q0:q1, :] for i in parts], axis=0)
        q = jnp.concatenate([q, q], axis=1)
        best = None
        for c in range(k0, k1, 128 * 3):
            kh = k_b[row, c : c + 384, :HD]
            kl = k_b[row, c : c + 384, HD:]
            x = dot_nt(q, jnp.concatenate([kh, kh, kl, kl], axis=1))
            s[: len(parts) * size, c : c + 384] = x
            for j in range(3):
                part = x[:, j * 128 : (j + 1) * 128]
                best = part if best is None else jnp.maximum(best, part)
        best = jnp.max(best, axis=1, keepdims=True)
        for n, i in enumerate(parts):
            own = slice(n * size, (n + 1) * size)
            old = peak[i, q0:q1, :]
            new = jnp.maximum(old, best[own])
            alpha[own, :] = jnp.exp2(old - new)
            top[own, :] = new
            peak[i, q0:q1, :] = new

    def gather(entry, double, tile, s, top, alpha):
        q0, q1, k0, k1 = tile
        size = q1 - q0
        row = entry >> 5
        parts = queries_of(entry, double)
        every = slice(0, len(parts) * size)
        high = top[every, :]
        part = None
        ps = []
        for c in range(k0, k1, 128):
            p = jnp.exp2(s[every, c : c + 128] - high)
            part = p if part is None else part + p
            ps.append(p)
        ph, pw = split_hi_lo(jnp.concatenate(ps, axis=1))
        v = v_b[row, k0:k1, :]
        pv = dot_nn(jnp.concatenate([ph, pw], axis=1), jnp.concatenate([v, v], axis=0))
        pv = pv[:, :HD] + pv[:, HD:]
        for n, i in enumerate(parts):
            own = slice(n * size, (n + 1) * size)
            scale = alpha[own, :]
            total[i, q0:q1, :] = total[i, q0:q1, :] * scale + part[own]
            acc[i, q0:q1, :] = acc[i, q0:q1, :] * scale + pv[own]

    even, odd = (s_0, m_0, a_0), (s_1, m_1, a_1)
    whole = (0, ROW, 0, KEYS)
    halves = [(w * TILE_SEG, (w + 1) * TILE_SEG, w * ROW, (w + 1) * ROW) for w in range(2)]

    @pl.when(wide & (n_twos > 0))
    def _():
        prepare(twos[0])
        score(twos[0], True, whole, *even)

        def step(g, carry):
            n = 2 * g
            here, then, later = twos[n], twos[n + 1], twos[n + 2]
            prepare(then)
            score(then, True, whole, *odd)
            gather(here, True, whole, *even)

            @pl.when(n + 1 < n_twos)
            def _():
                prepare(later)
                score(later, True, whole, *even)
                gather(then, True, whole, *odd)

            return carry

        lax.fori_loop(0, (n_twos + 1) >> 1, step, 0)

    @pl.when(wide)
    def _():
        def step(n, carry):
            here = ones[n]
            prepare(here)
            score(here, False, whole, *even)
            gather(here, False, whole, *even)
            return carry

        lax.fori_loop(0, n_ones, step, 0)

    @pl.when(jnp.logical_not(wide))
    def _():
        for entries, number, double in ((twos, n_twos, True), (ones, n_ones, False)):

            def step(n, carry):
                here = entries[n]
                prepare(here)
                for half, buffers in zip(halves, (even, odd)):
                    score(here, double, half, *buffers)
                for half, buffers in zip(halves, (even, odd)):
                    gather(here, double, half, *buffers)
                return carry

            lax.fori_loop(0, number, step, 0)

    def out_copies(i):
        if first:
            return [
                pltpu.make_async_copy(acc.at[i], outs[0].at[i], out_sem.at[0, i]),
                pltpu.make_async_copy(stat_0.at[i], outs[1].at[i], out_sem.at[1, i]),
            ]
        return [pltpu.make_async_copy(q_f.at[i], outs[0].at[i], out_sem.at[0, i])]

    if not first:
        for load in loads:
            load.wait()
    for i in range(4):
        weight = jnp.sum(total[i], axis=1, keepdims=True)
        if first:
            lane = lax.broadcasted_iota(jnp.int32, (ROW, HD), 1)
            stat_0[i] = jnp.where(lane < HD // 2, peak[i], weight)
        else:
            old = stat_0[i, :, :1]
            here = peak[i, :, :1]
            high = jnp.maximum(old, here)
            scale_0 = jnp.exp2(old - high)
            scale_1 = jnp.exp2(here - high)
            bottom = stat_0[i, :, HD // 2 : HD // 2 + 1] * scale_0 + weight * scale_1
            q_f[i] = (acc_0[i] * scale_0 + acc[i] * scale_1) / bottom
        for copy in out_copies(i):
            copy.start()
    for i in range(4):
        for copy in out_copies(i):
            copy.wait()


def attention(rows, sources, first, info, *arrays):
    n_rows = len(rows)
    hbm = pl.BlockSpec(memory_space=pl.ANY)
    n_out = 2 if first else 1
    state = pltpu.VMEM((4, ROW, HD), jnp.float32)
    column = pltpu.VMEM((2 * ROW, HD), jnp.float32)
    scores = pltpu.VMEM((2 * ROW, KEYS), jnp.float32)
    return pl.pallas_call(
        functools.partial(attention_kernel, rows, sources, first, len(arrays)),
        out_shape=[jax.ShapeDtypeStruct((4, ROW, HD), jnp.float32)] * n_out,
        in_specs=[pl.BlockSpec(memory_space=pltpu.SMEM)]
        + [hbm] * (1 if first else 3)
        + [pl.BlockSpec(memory_space=pltpu.VMEM)] * (len(arrays) - (1 if first else 3)),
        out_specs=[hbm] * n_out,
        scratch_shapes=[
            state,
            pltpu.VMEM((4, ROW, 2 * HD), jnp.bfloat16),
            pltpu.VMEM((n_rows, KEYS, 2 * HD), jnp.bfloat16),
            pltpu.VMEM((n_rows, KEYS, 2 * HD), jnp.bfloat16),
            state,
            state,
            state,
            state,
            state,
            scores,
            scores,
            column,
            column,
            column,
            column,
            pltpu.SMEM((n_rows * 2 + 2,), jnp.int32),
            pltpu.SMEM((n_rows + 1,), jnp.int32),
            pltpu.SemaphoreType.DMA,
            pltpu.SemaphoreType.DMA((2,)),
            pltpu.SemaphoreType.DMA((2, 4)),
        ],
        compiler_params=pltpu.CompilerParams(vmem_limit_bytes=(30 if first else 34) * 1024 * 1024),
        cost_estimate=pl.CostEstimate(flops=COST, bytes_accessed=8 * 2**20, transcendentals=0),
        name="own_rows" if first else "halo_rows",
    )(info, *arrays[: 1 if first else 3], *[pltpu.with_memory_space_constraint(x, pltpu.VMEM) for x in arrays[1 if first else 3 :]])


def own_sources(ins, row):
    t, h = OWN_ROWS[row]
    return [ins[1 + side].at[t, h] for side in range(2)]


def halo_sources(ins, row):
    t, h = HALO_ROWS[row]
    out = []
    for side in range(2):
        xm, xp, y, cm, cp = ins[3 + side * 5 : 8 + side * 5]
        if h < 2:
            out.append(xm.at[h] if t < 0 else xp.at[h])
        else:
            out.append(y.at[t] if t in (0, 1) else (cm if t < 0 else cp))
    return out


def body(queries, key_tokens, value_tokens, window_reach):
    yh = lax.axis_index("yh")
    head = lax.axis_index("zl") * 8 + (lax.axis_index("yl") ^ yh) * 4 + lax.axis_index("zh")
    reach = lax.dynamic_slice_in_dim(window_reach, head, 1, 0)[0]
    info = jnp.concatenate([jnp.minimum(reach, 1), lax.axis_index("x")[None]])

    def pieces(tensor):
        return tensor.reshape(BLOCK, HEADS, HD).transpose(1, 0, 2)

    def exchange(tensor):
        return lax.all_to_all(
            tensor, GROUP, split_axis=0, concat_axis=0, axis_index_groups=RANKS, tiled=True
        )

    def swap(tensor):
        return lax.ppermute(tensor, "core", [(0, 1), (1, 0)])

    up = [(i, i + 1) for i in range(3)]
    down = [(i + 1, i) for i in range(3)]
    across = [(i, 3 - i) for i in range(4)]

    both = jnp.stack([pieces(key_tokens), pieces(value_tokens)], axis=1)
    own, to_send, info = lax.optimization_barrier((exchange(both), pieces(queries), info))
    own = own.reshape(2, 2, 4, 2, BLOCK, HD)
    own_q = exchange(to_send).reshape(4, ROW, HD)

    xm = lax.ppermute(own[1], "x", up)
    xp = lax.ppermute(own[0], "x", down)
    edge = own[:, 1]
    y = lax.ppermute(edge, ("yh", "yl"), across)
    edge_up = [(i * 4 + j, (i + 1) * 4 + 3 - j) for i in range(3) for j in range(4)]
    edge_down = [((i + 1) * 4 + j, i * 4 + 3 - j) for i in range(3) for j in range(4)]
    cm = lax.ppermute(edge[1], ("x", "yh", "yl"), edge_up)
    cp = lax.ppermute(edge[0], ("x", "yh", "yl"), edge_down)
    halo = (xm, xp, y, cm, cp)
    state = attention(OWN_ROWS, own_sources, True, info, own_q, own, swap(own))
    state, halo = lax.optimization_barrier((state, halo))
    halo = halo + tuple(swap(part) for part in halo)
    (out,) = attention(HALO_ROWS, halo_sources, False, info, own_q, *state, *halo)
    back = exchange(out.reshape(HEADS, BLOCK, HD))
    return back.transpose(1, 0, 2).reshape(BLOCK, HEADS * HD)


def solution(mesh):
    fine = Mesh(mesh.devices.reshape(SIZES), AXES)
    spec = P(AXES, None)
    return jax.shard_map(
        body,
        mesh=fine,
        in_specs=(spec, spec, spec, P()),
        out_specs=spec,
        check_vma=False,
    )
```
